32 devices in a mesh: grp: 4 (over y, core), nbr: 8 (over z, x).
Axes of the slice: x: 2, y: 2, z: 4, core: 2. Of those that a mesh axis runs over, the one named last changes fastest.
Arguments:
- sims: float32 [512, 128, 128], P(('grp', 'nbr')), may hold values from -6 to 6
- own_tiles: float32 [6144, 128, 128], P(('grp', 'nbr')), may hold values from -0.15625 to 0.15625
- own_cols: int32 [6144], P(('grp', 'nbr')), may hold values from 0 to 143
- own_rows: int32 [6144], P(('grp', 'nbr')), may hold values from 0 to 15
- help_tiles: float32 [512, 128, 128], P(('grp', 'nbr')), may hold values from -0.15625 to 0.15625
- help_cols: int32 [512], P(('grp', 'nbr')), may hold values from 0 to 143
- help_rows: int32 [512], P(('grp', 'nbr')), may hold values from 0 to 15
- help_live: int32 [512], P(('grp', 'nbr')), may hold values from 0 to 1, as said below
Outputs:
- reobserved: float32 [512, 128, 128], P(('grp', 'nbr'))
The draws below stay inside these ranges and needn't reach their ends.
Inputs may be any that keep to these rules, and one draw needn't show every extreme that they name: `help_live`: helper slot j of a device serves the owner of neighbour index j // 2 in the same group, so at most 2 live slots go from one device to one owner; in every group one owner receives all 2 slots live from every device of the group.
All inputs are finite; a program needn't handle non-finite values.
Results may differ from the reference program's by a relative error of at most 0.0001.
Values sent between devices are 32-bit elements; how exact they have to be, the bound alone decides.
No kernel may reach another device: no remote copies, remote signals or barrier semaphores. Data moves between devices by JAX's collectives and lax.ppermute only.
A program may use at most 192 MiB of HBM per device.

```python
import jax
import jax.numpy as jnp
from jax import lax

TILE = 128
SIMS = 128
ROWS_DEV = 16
TILES_ROW = 12
CAP = 2
RIM = 8
GROUP_ROWS = 128
BLOCKS = 512
HELP_DEV = 16
N_GRP = 4
N_NBR = 8


def draw_help_live(key, part):
    devices = N_GRP * N_NBR
    base = jax.random.fold_in(key, 7)
    key_bits, key_owner = jax.random.split(base)
    bits = jax.random.randint(key_bits, (devices, N_NBR, CAP), 0, 2).astype(jnp.int32)
    chosen = jax.random.randint(key_owner, (N_GRP,), 0, N_NBR).astype(jnp.int32)
    forced = (jnp.arange(N_NBR, dtype=jnp.int32)[None, :] == chosen[:, None]).astype(jnp.int32)
    forced = jnp.repeat(forced, N_NBR, axis=0)
    live = jnp.maximum(bits, forced[:, :, None])
    return live.reshape(-1).astype(jnp.int32)


def touch_ends(entries, rng, smallest, largest):
    longest = entries.shape.index(max(entries.shape))
    spots = []
    for shift in (0, 1):
        where = [jax.random.randint(jax.random.fold_in(rng, axis), (), 0, length) for axis, length in enumerate(entries.shape)]
        where[longest] = (where[longest] + shift) % entries.shape[longest]
        spots.append(tuple(where))
    return entries.at[spots[0]].set(smallest).at[spots[1]].set(largest)


def shard_levels(key, dims, pieces, least, high):
    loudness = 1.0
    for position, blocks in pieces:
        heights = jax.random.uniform(jax.random.fold_in(jax.random.fold_in(key, 6), position), (blocks,), jnp.float32, least / len(pieces), high / len(pieces))
        loudness = loudness * jnp.repeat(jnp.exp(heights), dims[position] // blocks).reshape((-1,) + (1,) * (len(dims) - 1 - position))
    return loudness


def gaussian(stream_key, extent, scale, most, cuts=(), kind=jnp.bfloat16):
    values = scale * jax.random.normal(stream_key, extent, jnp.float32)
    if cuts:
        values = values * shard_levels(stream_key, extent, cuts, -0.22, 0.18)
    return jnp.clip(values, -most, most).astype(kind)


def setup_inputs(seed: int = 0) -> dict:
    arg_keys = jax.random.split(jax.random.key(seed), 9)
    return {
        "sims": gaussian(arg_keys[0], (BLOCKS, TILE, SIMS), 1.0, 6.0, ((0, 32),), jnp.float32),
        "own_tiles": gaussian(arg_keys[1], (BLOCKS * TILES_ROW, TILE, TILE), (TILE * TILES_ROW) ** -0.5, 0.15625, ((0, 32),), jnp.float32),
        "own_cols": touch_ends(jax.random.randint(arg_keys[2], (BLOCKS * TILES_ROW,), 0, GROUP_ROWS + 2 * RIM), jax.random.fold_in(arg_keys[2], 1), 0, (GROUP_ROWS + 2 * RIM) - 1).astype(jnp.int32),
        "own_rows": touch_ends(jax.random.randint(arg_keys[3], (BLOCKS * TILES_ROW,), 0, ROWS_DEV), jax.random.fold_in(arg_keys[3], 1), 0, ROWS_DEV - 1).astype(jnp.int32),
        "help_tiles": gaussian(arg_keys[4], (BLOCKS // ROWS_DEV * HELP_DEV, TILE, TILE), (TILE * TILES_ROW) ** -0.5, 0.15625, ((0, 32),), jnp.float32),
        "help_cols": touch_ends(jax.random.randint(arg_keys[5], (BLOCKS // ROWS_DEV * HELP_DEV,), 0, GROUP_ROWS + 2 * RIM), jax.random.fold_in(arg_keys[5], 1), 0, (GROUP_ROWS + 2 * RIM) - 1).astype(jnp.int32),
        "help_rows": touch_ends(jax.random.randint(arg_keys[6], (BLOCKS // ROWS_DEV * HELP_DEV,), 0, ROWS_DEV), jax.random.fold_in(arg_keys[6], 1), 0, ROWS_DEV - 1).astype(jnp.int32),
        "help_live": draw_help_live(jax.random.fold_in(arg_keys[8], 71), 0),
    }


def reference(sims, own_tiles, own_cols, own_rows, help_tiles, help_cols, help_rows, help_live):
    devices = N_GRP * N_NBR
    group_rows = ROWS_DEV * N_NBR
    tile_dev = ROWS_DEV * TILES_ROW
    help_dev = N_NBR * CAP
    padded = jnp.pad(sims, ((RIM, RIM), (0, 0), (0, 0)))
    high = lax.Precision.HIGHEST

    def visit(device, total):
        group = device // N_NBR
        extended = lax.dynamic_slice_in_dim(padded, (group * group_rows).astype(jnp.int32), group_rows + 2 * RIM, 0)
        tiles = lax.dynamic_slice_in_dim(own_tiles, (device * tile_dev).astype(jnp.int32), tile_dev, 0)
        cols = lax.dynamic_slice_in_dim(own_cols, (device * tile_dev).astype(jnp.int32), tile_dev, 0)
        rows = lax.dynamic_slice_in_dim(own_rows, (device * tile_dev).astype(jnp.int32), tile_dev, 0)
        picked = jnp.take(extended, cols, axis=0)
        terms = jnp.einsum("tij,tjs->tis", tiles, picked, precision=high)
        select = (rows[None, :] == jnp.arange(ROWS_DEV, dtype=jnp.int32)[:, None]).astype(jnp.float32)
        own_sum = jnp.einsum("rt,tis->ris", select, terms, precision=high)
        start = (device * ROWS_DEV).astype(jnp.int32)
        block = lax.dynamic_slice_in_dim(total, start, ROWS_DEV, 0)
        total = lax.dynamic_update_slice_in_dim(total, block + own_sum, start, 0)
        htiles = lax.dynamic_slice_in_dim(help_tiles, (device * help_dev).astype(jnp.int32), help_dev, 0)
        hcols = lax.dynamic_slice_in_dim(help_cols, (device * help_dev).astype(jnp.int32), help_dev, 0)
        hrows = lax.dynamic_slice_in_dim(help_rows, (device * help_dev).astype(jnp.int32), help_dev, 0)
        hlive = lax.dynamic_slice_in_dim(help_live, (device * help_dev).astype(jnp.int32), help_dev, 0)
        hpicked = jnp.take(extended, hcols, axis=0)
        hterms = jnp.einsum("tij,tjs->tis", htiles, hpicked, precision=high)
        hterms = hterms * hlive.astype(jnp.float32)[:, None, None]
        target = (jnp.arange(help_dev, dtype=jnp.int32) // CAP) * ROWS_DEV + hrows
        hselect = (target[None, :] == jnp.arange(group_rows, dtype=jnp.int32)[:, None]).astype(jnp.float32)
        help_sum = jnp.einsum("rt,tis->ris", hselect, hterms, precision=high)
        gstart = (group * group_rows).astype(jnp.int32)
        gblock = lax.dynamic_slice_in_dim(total, gstart, group_rows, 0)
        return lax.dynamic_update_slice_in_dim(total, gblock + help_sum, gstart, 0)

    total = jnp.zeros(sims.shape, jnp.float32)
    return lax.fori_loop(0, devices, visit, total)
```

```python
import functools

import jax
import jax.numpy as jnp
import numpy as np
from jax import lax
from jax.experimental import pallas as pl
from jax.experimental.pallas import tpu as pltpu
from jax.sharding import PartitionSpec as P

RIM = 8
UNROLL = 4
DEPTH = 4
VMEM_BYTES = 40 << 20
HIGH = lax.Precision.HIGHEST
F32 = jnp.float32
I32 = jnp.int32


def grid_of(mesh):
    count = mesh.shape["nbr"]
    try:
        where = np.array([d.coords for d in mesh.devices[0]])
    except AttributeError:
        return [(i, 0) for i in range(count)]
    axes = [a for a in range(where.shape[1]) if len(set(where[:, a])) > 1]
    if len(axes) != 2:
        return [(i, 0) for i in range(count)]
    first, second = axes
    if len(set(where[:, second])) > len(set(where[:, first])):
        first, second = second, first
    where = where - where.min(axis=0)
    return [(int(w[first]), int(w[second])) for w in where]


def ring_of(places):
    index = {place: n for n, place in enumerate(places)}
    rows = max(p[0] for p in places) + 1
    cols = max(p[1] for p in places) + 1
    if len(index) != rows * cols or rows % 2 or cols < 2:
        return list(range(len(places)))
    walk = [(r, 0) for r in range(rows)]
    for step, r in enumerate(reversed(range(rows))):
        across = range(1, cols) if step % 2 == 0 else reversed(range(1, cols))
        walk += [(r, c) for c in across]
    return [index[w] for w in walk]


class Plan:
    def __init__(self, mesh):
        self.groups = mesh.shape["grp"]
        self.count = mesh.shape["nbr"]
        places = grid_of(mesh)
        self.ring = ring_of(places)
        self.pos = [self.ring.index(n) for n in range(self.count)]
        self.half = self.count // 2
        count, half = self.count, self.half
        self.right = self.around([(i, (i + 1) % count) for i in range(count)])
        self.left = self.around([(i, (i - 1) % count) for i in range(count)])
        near = lambda a, b: sum(abs(u - v) for u, v in zip(places[self.ring[a]], places[self.ring[b]])) == 1
        self.cross_r, self.cross_l = {}, {}
        for i in range(count):
            over_r, over_l = (i + half + 1) % count, (i + half - 1) % count
            if half > 2 and near(i, over_r) and over_r not in self.cross_r.values():
                self.cross_r[i] = over_r
            elif half > 2 and near(i, over_l) and over_l not in self.cross_l.values():
                self.cross_l[i] = over_l
        self.ends = [i for i in range(count) if i not in self.cross_r and i not in self.cross_l]
        self.pairs_r = self.around([(s, i) for i, s in self.cross_r.items()])
        self.pairs_l = self.around([(s, i) for i, s in self.cross_l.items()])
        self.end_right = self.around([((i - 1) % count, i) for i in self.ends])
        self.end_left = self.around([((i + 1) % count, i) for i in self.ends])

    def around(self, pairs):
        return [(self.ring[a], self.ring[b]) for a, b in pairs]

    def between(self, step, keep):
        return [
            (g * self.count + self.ring[i], (g + step) * self.count + self.ring[i])
            for g in range(self.groups)
            if 0 <= g + step < self.groups
            for i in keep
        ]


def copy_in(pieces, place, sem):
    return [
        pltpu.make_async_copy(ref, place.at[pl.ds(at, ref.shape[0])], sem.at[k])
        for k, (ref, at) in enumerate(pieces)
    ]


def run_tiles(offs, info, stage, bits, tiles, xs, acc, buf, sems, ready):
    slot_bits, row_bits = bits
    total = info.shape[0]
    dump = acc.shape[0] - 1
    first, last = offs[stage], offs[stage + 1]
    groups = lax.div(last - first + (UNROLL - 1), UNROLL)

    def fetch(g):
        s = lax.rem(g, DEPTH)
        for u in range(UNROLL):
            at = jnp.minimum(first + g * UNROLL + u, total - 1)
            tile = lax.shift_right_logical(info[at], slot_bits + row_bits)
            pltpu.make_async_copy(tiles.at[tile], buf.at[s, u], sems.at[s]).start()

    for g in range(DEPTH - 1):
        pl.when(g < groups)(functools.partial(fetch, jnp.int32(g)))
    ready()

    def body(g, carry):
        s = lax.rem(g, DEPTH)
        pl.when(g + DEPTH - 1 < groups)(lambda: fetch(g + DEPTH - 1))
        for u in range(UNROLL):
            pltpu.make_async_copy(tiles.at[0], buf.at[s, u], sems.at[s]).wait()
        rows, terms = [], []
        for u in range(UNROLL):
            at = first + g * UNROLL + u
            entry = info[jnp.minimum(at, total - 1)]
            row = lax.shift_right_logical(entry, slot_bits) & ((1 << row_bits) - 1)
            slot = entry & ((1 << slot_bits) - 1)
            rows.append(jnp.where(at < last, row, dump))
            terms.append(jnp.dot(buf[s, u], xs[slot], precision=HIGH, preferred_element_type=F32))
        for row, term in zip(rows, terms):
            acc[row] += term
        return carry

    lax.fori_loop(0, groups, body, 0)


def stage_kernel(stage, bits, have, offs, info, *refs):
    refs = list(refs)
    shards = [refs.pop(0) for _ in range(have)]
    tiles = refs.pop(0)
    before = refs.pop(0) if stage else None
    acc, xs, buf, xsems, sems = refs
    starts = np.cumsum([0] + [s.shape[0] for s in shards])
    copies = copy_in(list(zip(shards, starts)), xs, xsems)
    for c in copies:
        c.start()

    def ready():
        acc[...] = jnp.zeros_like(acc) if before is None else before[...]
        for c in copies:
            c.wait()

    run_tiles(offs, info, stage, bits, tiles, xs, acc, buf, sems, ready)


def last_stage_kernel(stage, bits, rows, modes, offs, info, mode, hbuf, hidx, *refs):
    refs = list(refs)
    sources = [refs.pop(0) for _ in range(len(refs) - 8)]
    tiles, before, acc, hx, xs, buf, xsems, sems = refs
    far_a, far_b, far_r, far_l, low_near, low_far, up_near, up_far = sources[-8:]
    half = far_a.shape[0]
    slots = hx.shape[0]

    def gather(j, carry):
        for k, source in enumerate(sources):
            @pl.when(hbuf[j] == k)
            def _():
                pltpu.make_async_copy(source.at[hidx[j]], hx.at[j], xsems.at[4]).start()
        return carry

    lax.fori_loop(0, slots, gather, 0)

    def bring(ref, at, k):
        pltpu.make_async_copy(ref, xs.at[pl.ds(at, ref.shape[0])], xsems.at[k]).start()

    @pl.when(mode[0] == 0)
    def _():
        bring(far_a, 0, 0)
        bring(far_b, half, 1)

    @pl.when(mode[0] == 1)
    def _():
        bring(far_r.at[pl.ds(0, half)], 0, 0)
        bring(far_r.at[pl.ds(half, half)], half, 1)

    @pl.when(mode[0] == 2)
    def _():
        bring(far_l.at[pl.ds(0, half)], 0, 0)
        bring(far_l.at[pl.ds(half, half)], half, 1)

    @pl.when(mode[1] == 0)
    def _():
        bring(low_near, rows, 2)

    @pl.when(mode[1] == 1)
    def _():
        bring(low_far, rows, 2)

    @pl.when(mode[2] == 0)
    def _():
        bring(up_near, rows + RIM, 3)

    @pl.when(mode[2] == 1)
    def _():
        bring(up_far, rows + RIM, 3)

    def ready():
        acc[...] = before[...]
        pltpu.make_async_copy(far_a, xs.at[pl.ds(0, half)], xsems.at[0]).wait()
        pltpu.make_async_copy(far_b, xs.at[pl.ds(half, half)], xsems.at[1]).wait()
        pltpu.make_async_copy(low_near, xs.at[pl.ds(rows, RIM)], xsems.at[2]).wait()
        pltpu.make_async_copy(up_near, xs.at[pl.ds(rows + RIM, RIM)], xsems.at[3]).wait()

    run_tiles(offs, info, stage, bits, tiles, xs, acc, buf, sems, ready)

    def drain(j, carry):
        pltpu.make_async_copy(sources[0].at[0], hx.at[j], xsems.at[4]).wait()
        return carry

    lax.fori_loop(0, slots, drain, 0)


def help_kernel(hrow, tiles, xs, before, out, acc):
    rows = out.shape[0]
    acc[...] = before[...]

    def body(g, carry):
        terms = []
        for u in range(2):
            j = g * 2 + u
            terms.append(jnp.dot(tiles[j], xs[j], precision=HIGH, preferred_element_type=F32))
        for u in range(2):
            acc[hrow[g * 2 + u]] += terms[u]
        return carry

    lax.fori_loop(0, tiles.shape[0] // 2, body, 0)
    if tiles.shape[0] % 2:
        j = tiles.shape[0] - 1
        acc[hrow[j]] += jnp.dot(tiles[j], xs[j], precision=HIGH, preferred_element_type=F32)
    out[...] = acc[pl.ds(0, rows)]


def edge_kernel(count, mode, *refs):
    refs = list(refs)
    low, up, sems = refs[-3:]
    shards = refs[:-3]
    size = shards[0].shape[0]

    def pick(k, ref):
        @pl.when(mode[3] == k)
        def _():
            pltpu.make_async_copy(ref.at[pl.ds(size - RIM, RIM)], low, sems.at[0]).start()

        @pl.when(mode[4] == k)
        def _():
            pltpu.make_async_copy(ref.at[pl.ds(0, RIM)], up, sems.at[1]).start()

    for k, ref in enumerate(shards):
        pick(k, ref)
    pltpu.make_async_copy(shards[0].at[pl.ds(0, RIM)], low, sems.at[0]).wait()
    pltpu.make_async_copy(shards[0].at[pl.ds(0, RIM)], up, sems.at[1]).wait()


def bits_for(n):
    return max(1, (n - 1).bit_length())


SMEM = pl.BlockSpec(memory_space=pltpu.SMEM)
ANY = pl.BlockSpec(memory_space=pl.ANY)
VMEM = pl.BlockSpec(memory_space=pltpu.VMEM)


def local(plan, sims, own_tiles, own_cols, own_rows, help_tiles, help_cols, help_rows, help_live):
    rows, side, width = sims.shape
    count, half = plan.count, plan.half
    group_rows = rows * count
    cut = rows // 2
    total = own_tiles.shape[0]
    slots = help_tiles.shape[0]
    per_stage = max(2 * rows, rows + 2 * RIM)
    bits = (bits_for(per_stage), bits_for(rows))
    both = ("grp", "nbr")

    me = lax.axis_index("nbr")
    table = lambda values, index: sum(
        jnp.where(index == k, I32(v), I32(0)) for k, v in enumerate(values)
    )
    here = table(plan.pos, me)

    from_left, from_right = [sims], [sims]
    for _ in range(1, half):
        from_left.append(lax.ppermute(from_left[-1], "nbr", plan.right))
        from_right.append(lax.ppermute(from_right[-1], "nbr", plan.left))
    far_r = lax.ppermute(from_left[1], "nbr", plan.pairs_r)
    far_l = lax.ppermute(from_right[1], "nbr", plan.pairs_l)
    far_a = lax.ppermute(from_left[-1][:cut], "nbr", plan.end_right)
    far_b = lax.ppermute(from_right[-1][cut:], "nbr", plan.end_left)

    notes = jnp.stack([help_cols, help_rows, help_live], axis=1)
    notes = lax.all_to_all(notes, "nbr", split_axis=0, concat_axis=0, tiled=True)
    in_tiles = lax.all_to_all(help_tiles, "nbr", split_axis=0, concat_axis=0, tiled=True)

    kind_of = lambda members, value: [value if i in members else 0 for i in range(count)]
    far_kind = table([a + b for a, b in zip(kind_of(plan.cross_r, 1), kind_of(plan.cross_l, 2))], here)
    place_low, place_up = plan.pos[count - 1], plan.pos[0]

    def locate(cols):
        block = cols - RIM
        low, up = block < 0, block >= group_rows
        inside = jnp.clip(block, 0, group_rows - 1)
        shard = inside // rows
        index = inside - shard * rows
        ahead = lax.rem(table(plan.pos, shard) - here + count, I32(count))
        stage = jnp.minimum(ahead, count - ahead)
        from_right_side = (ahead > 0) & (ahead < half)
        slot = index + jnp.where(from_right_side, rows, 0)
        rim = low | up
        slot = jnp.where(low, rows + cols, jnp.where(up, rows + RIM + block - group_rows, slot))
        stage = jnp.where(rim, half, stage)
        near_buf = jnp.where(ahead == 0, 0, jnp.where(ahead < half, half - 1 + ahead, count - ahead))
        base = 2 * half - 1
        far_buf = jnp.where(
            far_kind == 0, jnp.where(index < cut, base, base + 1), jnp.where(far_kind == 1, base + 2, base + 3)
        )
        far_idx = jnp.where((far_kind == 0) & (index >= cut), index - cut, index)
        far = ahead == half
        buf = jnp.where(far, far_buf, near_buf)
        idx = jnp.where(far, far_idx, index)
        buf = jnp.where(low, base + 4 + low_far_kind, jnp.where(up, base + 6 + up_far_kind, buf))
        idx = jnp.where(low, cols, jnp.where(up, block - group_rows, idx))
        return stage, slot, buf, idx

    def away(place):
        return lax.rem(I32(place) - here + count, I32(count))

    low_far_kind = (away(place_low) == half).astype(I32)
    up_far_kind = (away(place_up) == half).astype(I32)

    def edge_source(place):
        ahead = away(place)
        near = jnp.where(ahead == 0, 0, jnp.where(ahead < half, half - 1 + ahead, count - ahead))
        return jnp.where(ahead == half, 0, near)

    mode = jnp.stack(
        [far_kind, low_far_kind, up_far_kind, edge_source(place_low), edge_source(place_up)]
    ).astype(I32)

    stage, slot, _, _ = locate(own_cols)
    number = jnp.arange(total, dtype=I32)
    key = (stage * per_stage + slot) * total + number
    rank = jnp.sum((key[None, :] < key[:, None]).astype(I32), axis=1)
    entry = (number << (bits[0] + bits[1])) | (own_rows << bits[0]) | slot
    info = jnp.sum(jnp.where(rank[:, None] == number[None, :], entry[:, None], 0), axis=0)
    offs = jnp.sum(
        (stage[None, :] < jnp.arange(half + 2, dtype=I32)[:, None]).astype(I32), axis=1
    )

    _, _, hbuf, hidx = locate(notes[:, 0])
    hrow = jnp.where(notes[:, 2] > 0, notes[:, 1], rows)

    partial = jax.ShapeDtypeStruct((rows + 1, side, width), F32)
    scratch = lambda more: [
        pltpu.VMEM((per_stage, side, width), F32),
        pltpu.VMEM((DEPTH, UNROLL, side, side), F32),
        pltpu.SemaphoreType.DMA((more,)),
        pltpu.SemaphoreType.DMA((DEPTH,)),
    ]
    params = pltpu.CompilerParams(vmem_limit_bytes=VMEM_BYTES)
    cost = pl.CostEstimate(
        flops=2 * side * side * width * total // count, bytes_accessed=8 << 20, transcendentals=0
    )
    acc = None
    for s in range(half):
        shards = [sims] if s == 0 else [from_left[s], from_right[s]]
        args = [offs, info, *shards, own_tiles] + ([] if s == 0 else [acc])
        acc = pl.pallas_call(
            functools.partial(stage_kernel, s, bits, len(shards)),
            out_shape=partial,
            in_specs=[SMEM, SMEM] + [ANY] * (len(shards) + 1) + ([] if s == 0 else [VMEM]),
            out_specs=VMEM,
            scratch_shapes=scratch(2),
            compiler_params=params,
            cost_estimate=cost,
            name=f"stage{s}",
        )(*args)

    near_shards = [sims] + from_left[1:] + from_right[1:]
    edge = jax.ShapeDtypeStruct((RIM, side, width), F32)
    edge_low, edge_up = pl.pallas_call(
        functools.partial(edge_kernel, count),
        out_shape=(edge, edge),
        in_specs=[SMEM] + [ANY] * len(near_shards),
        out_specs=(ANY, ANY),
        scratch_shapes=[pltpu.SemaphoreType.DMA((2,))],
        name="edges",
    )(mode, *near_shards)
    far_low, far_up = (place_low + half) % count, (place_up + half) % count
    without = lambda i: [k for k in range(count) if k != i]
    low_near = lax.ppermute(edge_low, both, plan.between(1, without(far_low)))
    up_near = lax.ppermute(edge_up, both, plan.between(-1, without(far_up)))

    def far_shard(i, tail):
        if i in plan.cross_r or i in plan.cross_l:
            whole = far_r if i in plan.cross_r else far_l
        elif cut >= RIM:
            whole = far_b if tail else far_a
        else:
            whole = jnp.concatenate([far_a, far_b], axis=0)
        return whole[whole.shape[0] - RIM :] if tail else whole[:RIM]

    low_far = lax.ppermute(far_shard(far_low, True), both, plan.between(1, [far_low]))
    up_far = lax.ppermute(far_shard(far_up, False), both, plan.between(-1, [far_up]))

    sources = near_shards + [far_a, far_b, far_r, far_l, low_near, low_far, up_near, up_far]
    acc, hx = pl.pallas_call(
        functools.partial(last_stage_kernel, half, bits, rows, None),
        out_shape=(partial, jax.ShapeDtypeStruct((slots, side, width), F32)),
        in_specs=[SMEM] * 5 + [ANY] * (len(sources) + 1) + [VMEM],
        out_specs=(VMEM, ANY),
        scratch_shapes=scratch(5),
        compiler_params=params,
        cost_estimate=cost,
        name="last_stage",
    )(offs, info, mode, hbuf, hidx, *sources, own_tiles, acc)

    return pl.pallas_call(
        help_kernel,
        out_shape=jax.ShapeDtypeStruct((rows, side, width), F32),
        in_specs=[SMEM, VMEM, VMEM, VMEM],
        out_specs=VMEM,
        scratch_shapes=[pltpu.VMEM((rows + 1, side, width), F32)],
        compiler_params=params,
        name="help",
    )(hrow, in_tiles, hx, acc)


def solution(mesh):
    spread = P(("grp", "nbr"), None, None)
    flat = P(("grp", "nbr"))
    return jax.shard_map(
        functools.partial(local, Plan(mesh)),
        mesh=mesh,
        in_specs=(spread, spread, flat, flat, spread, flat, flat, flat),
        out_specs=spread,
        check_vma=False,
    )
```

```python
import functools

import jax
import jax.numpy as jnp
import numpy as np
from jax import lax
from jax.experimental import pallas as pl
from jax.experimental.pallas import tpu as pltpu
from jax.sharding import PartitionSpec as P

RIM = 8
UNROLL = 8
NOTE_ROWS = 8
FAR_PLACE, CUTS, OVER, RIM_FROM, LAST = 4, 6, 10, 12, 14
DEPTH = 4
VMEM_BYTES = 42 << 20
F32 = jnp.float32
I32 = jnp.int32


def grid_of(mesh):
    count = mesh.shape["nbr"]
    try:
        where = np.array([d.coords for d in mesh.devices[0]])
    except AttributeError:
        return [(i, 0) for i in range(count)]
    axes = [a for a in range(where.shape[1]) if len(set(where[:, a])) > 1]
    if len(axes) != 2:
        return [(i, 0) for i in range(count)]
    first, second = axes
    if len(set(where[:, second])) > len(set(where[:, first])):
        first, second = second, first
    where = where - where.min(axis=0)
    return [(int(w[first]), int(w[second])) for w in where]


def ring_of(places):
    index = {place: n for n, place in enumerate(places)}
    rows = max(p[0] for p in places) + 1
    cols = max(p[1] for p in places) + 1
    if len(index) != rows * cols or rows % 2 or cols < 2:
        return list(range(len(places)))
    walk = [(r, 0) for r in range(rows)]
    for step, r in enumerate(reversed(range(rows))):
        across = range(1, cols) if step % 2 == 0 else reversed(range(1, cols))
        walk += [(r, c) for c in across]
    return [index[w] for w in walk]


class Plan:
    def __init__(self, mesh):
        self.groups = mesh.shape["grp"]
        self.count = mesh.shape["nbr"]
        places = grid_of(mesh)
        self.ring = ring_of(places)
        self.pos = [self.ring.index(n) for n in range(self.count)]
        self.half = self.count // 2
        count, half = self.count, self.half
        self.right = self.around([(i, (i + 1) % count) for i in range(count)])
        self.left = self.around([(i, (i - 1) % count) for i in range(count)])
        near = lambda a, b: sum(abs(u - v) for u, v in zip(places[self.ring[a]], places[self.ring[b]])) == 1
        pairs, self.over_r, self.over_l, self.from_right = [], [], [], []
        for i in range(count) if half > 3 else ():
            for members, j in ((self.over_r, (i + 3) % count), (self.over_l, (i - 3) % count)):
                if near(i, j) and all(i != b and j != a for a, b in pairs):
                    pairs.append((j, i))
                    members.append(i)
                    self.from_right += [j] if members is self.over_r else []
        self.over = self.around(pairs)
        self.last_right = self.around([((i - 1) % count, i) for i in range(count) if i not in self.over_r])
        self.last_left = self.around([((i + 1) % count, i) for i in range(count) if i not in self.over_l])

    def around(self, pairs):
        return [(self.ring[a], self.ring[b]) for a, b in pairs]

    def between(self, step, keep):
        return [
            (g * self.count + self.ring[i], (g + step) * self.count + self.ring[i])
            for g in range(self.groups)
            if 0 <= g + step < self.groups
            for i in keep
        ]


def product(a, b):
    a_hi, b_hi = a.astype(jnp.bfloat16), b.astype(jnp.bfloat16)
    a_lo = (a - a_hi.astype(F32)).astype(jnp.bfloat16)
    b_lo = (b - b_hi.astype(F32)).astype(jnp.bfloat16)
    dot = functools.partial(jnp.dot, preferred_element_type=F32)
    return dot(a_hi, b_hi) + (dot(a_lo, b_hi) + dot(a_hi, b_lo))


def run_list(offs, info, stage, bits, fetch_tile, xs, acc, buf, sems, ready):
    slot_bits, row_bits = bits
    total = info.shape[0]
    dump = acc.shape[0] - 1
    first, last = offs[stage], offs[stage + 1]
    groups = lax.div(last - first + (UNROLL - 1), UNROLL)

    def fetch(g):
        s = lax.rem(g, DEPTH)
        for u in range(UNROLL):
            at = jnp.minimum(first + g * UNROLL + u, total - 1)
            fetch_tile(lax.shift_right_logical(info[at], slot_bits + row_bits), buf.at[s, u], sems.at[s]).start()

    for g in range(DEPTH - 1):
        pl.when(g < groups)(functools.partial(fetch, jnp.int32(g)))
    ready()

    def body(g, carry):
        s = lax.rem(g, DEPTH)
        pl.when(g + DEPTH - 1 < groups)(lambda: fetch(g + DEPTH - 1))
        for u in range(UNROLL):
            fetch_tile(0, buf.at[s, u], sems.at[s]).wait()
        rows, terms = [], []
        for u in range(UNROLL):
            at = first + g * UNROLL + u
            entry = info[jnp.minimum(at, total - 1)]
            row = lax.shift_right_logical(entry, slot_bits) & ((1 << row_bits) - 1)
            slot = jnp.where(at < last, entry & ((1 << slot_bits) - 1), 0)
            rows.append(jnp.where(at < last, row, dump))
            terms.append(product(buf[s, u], xs[slot]))
        for row, term in zip(rows, terms):
            acc[row] += term
        return carry

    lax.fori_loop(0, groups, body, 0)


def stage_kernel(stage, bits, layout, helped, *refs):
    refs = list(refs)
    offs, info = refs.pop(0), refs.pop(0)
    hoffs, hinfo = (refs.pop(0), refs.pop(0)) if helped else (None, None)
    mode = refs.pop(0)
    sources = [refs.pop(0) for _ in range(1 + max(c[1] for place in layout for c in place[2]))]
    tiles = refs.pop(0)
    received = refs.pop(0) if helped else None
    before = refs.pop(0) if stage else None
    out, acc, xs, buf, hbuf, xsems, sems, hsems = refs
    rows = acc.shape[0] - 1
    kept = out.shape[0]

    def bring(at, source, start, size, sem):
        return pltpu.make_async_copy(sources[source].at[pl.ds(start, size)], xs.at[pl.ds(at, size)], sem)

    back = None
    if before is not None:
        back = pltpu.make_async_copy(before, acc.at[pl.ds(0, rows)], xsems.at[len(layout)])
        back.start()
    def place_of(at):
        return at if isinstance(at, int) else at[0] + mode[at[1]] * at[2]

    for k, (at, which, choices) in enumerate(layout):
        for value, source, start, size in choices:
            start_it = bring(place_of(at), source, start, size, xsems.at[k]).start
            if which is None:
                start_it()
            else:
                pl.when(mode[which] == value)(start_it)

    def ready():
        if back is None:
            acc[...] = jnp.zeros_like(acc)
        else:
            back.wait()
        for k, (at, _, choices) in enumerate(layout):
            _, source, start, size = choices[0]
            bring(place_of(at), source, start, size, xsems.at[k]).wait()

    def own_tile(t, place, sem):
        return pltpu.make_async_copy(tiles.at[t], place, sem)

    side = tiles.shape[1]

    def help_tile(t, place, sem):
        per = (received.shape[1] - NOTE_ROWS) // side
        chunk = lax.div(t, per)
        start = pl.multiple_of((t - chunk * per) * side, side)
        return pltpu.make_async_copy(received.at[chunk, pl.ds(start, side)], place, sem)

    run_list(offs, info, stage, bits, own_tile, xs, acc, buf, sems, ready)
    if helped:
        run_list(hoffs, hinfo, stage, bits, help_tile, xs, acc, hbuf, hsems, lambda: None)
    out[...] = acc[pl.ds(0, kept)]


def edge_kernel(mode, *refs):
    refs = list(refs)
    low, up, sems = refs[-3:]
    shards = refs[:-4]
    size = shards[0].shape[0]
    for which, out, sem in ((2, low, sems.at[0]), (3, up, sems.at[1])):
        pl.when(mode[which] < 0)(pltpu.make_async_copy(shards[0].at[pl.ds(0, RIM)], out, sem).start)

    def pick(k, ref):
        @pl.when(mode[2] == k)
        def _():
            pltpu.make_async_copy(ref.at[pl.ds(size - RIM, RIM)], low, sems.at[0]).start()

        @pl.when(mode[3] == k)
        def _():
            pltpu.make_async_copy(ref.at[pl.ds(0, RIM)], up, sems.at[1]).start()

    for k, ref in enumerate(shards):
        pick(k, ref)
    pltpu.make_async_copy(shards[0].at[pl.ds(0, RIM)], low, sems.at[0]).wait()
    pltpu.make_async_copy(shards[0].at[pl.ds(0, RIM)], up, sems.at[1]).wait()


def cut_kernel(mode, *refs):
    *shards, first, second, rim, sems = refs
    half = first.shape[0]
    outs = [(first, mode[CUTS], mode[CUTS + 1] * half), (second, mode[CUTS + 2], mode[CUTS + 3] * half)]
    outs.append((rim, jnp.maximum(mode[RIM_FROM], 0), mode[RIM_FROM + 1]))
    for k, (out, which, start) in enumerate(outs):
        for value, ref in enumerate(shards):
            copy = pltpu.make_async_copy(ref.at[pl.ds(start, out.shape[0])], out, sems.at[k])
            pl.when(which == value)(copy.start)
    for k, (out, _, _) in enumerate(outs):
        pltpu.make_async_copy(shards[0].at[pl.ds(0, out.shape[0])], out, sems.at[k]).wait()


def bits_for(n):
    return max(1, (n - 1).bit_length())


SMEM = pl.BlockSpec(memory_space=pltpu.SMEM)
ANY = pl.BlockSpec(memory_space=pl.ANY)
VMEM = pl.BlockSpec(memory_space=pltpu.VMEM)


def table(values, index):
    return sum(jnp.where(index == k, I32(v), I32(0)) for k, v in enumerate(values))


def listed(stage, slot, row, stages, per_stage, bits, kept=None):
    place = stage * per_stage + slot
    rest = (row << bits[0]) | slot
    if kept is not None:
        place, rest = (x[:, :kept].reshape(-1) for x in (place, rest))
    total = place.shape[0]
    number = jnp.arange(total, dtype=I32)
    key = place * total + number
    rank = jnp.sum((key[None, :] < key[:, None]).astype(I32), axis=1)
    entry = (number << (bits[0] + bits[1])) | rest
    info = jnp.sum(jnp.where(rank[:, None] == number[None, :], entry[:, None], 0), axis=0)
    starts = jnp.arange(stages + 1, dtype=I32) * per_stage
    offs = jnp.sum((place[None, :] < starts[:, None]).astype(I32), axis=1)
    return offs, info


def local(plan, sims, own_tiles, own_cols, own_rows, help_tiles, help_cols, help_rows, help_live):
    rows, side, width = sims.shape
    count, half = plan.count, plan.half
    group_rows = rows * count
    cut = rows // 2
    assert rows == 2 * cut and cut >= RIM
    slots = help_tiles.shape[0]
    per_owner = slots // count
    join = min(3, half - 1)
    per_stage = (2 * join + 1) * rows + 2 * RIM
    bits = (bits_for(per_stage), bits_for(rows))
    both = ("grp", "nbr")
    here = table(plan.pos, lax.axis_index("nbr"))

    notes = jnp.stack([help_cols, help_rows, help_live], axis=0).astype(F32).reshape(3, count, per_owner)
    notes = jnp.pad(notes.transpose(1, 0, 2), ((0, 0), (0, NOTE_ROWS - 3), (0, width - per_owner)))
    sent = jnp.concatenate([help_tiles.reshape(count, per_owner * side, width), notes], axis=1)
    received = lax.all_to_all(sent, "nbr", split_axis=0, concat_axis=0, tiled=True)

    place_low, place_up = plan.pos[count - 1], plan.pos[0]

    def away(place):
        return lax.rem(I32(place) - here + count, I32(count))

    low_far = (away(place_low) == half).astype(I32)
    up_far = (away(place_up) == half).astype(I32)

    def locate(cols, least):
        block = cols - RIM
        low, up = block < 0, block >= group_rows
        inside = jnp.clip(block, 0, group_rows - 1)
        shard = inside // rows
        ahead = lax.rem(table(plan.pos, shard) - here + count, I32(count))
        near = jnp.minimum(ahead, count - ahead)
        stage = jnp.maximum(near, least)
        right = ((ahead > 0) & (ahead < half)).astype(I32)
        order = jnp.where(stage == join, jnp.where(near == 0, 0, 2 * near - 1 + right), right)
        slot = inside - shard * rows + order * rows
        slot = jnp.where(low, rows + cols, jnp.where(up, rows + RIM + block - group_rows, slot))
        stage = jnp.where(low, half + low_far, jnp.where(up, half + up_far, stage))
        return stage, slot

    over_r_kind = table([int(i in plan.over_r) for i in range(count)], here)
    over_l_kind = table([int(i in plan.over_l) for i in range(count)], here)

    def edge_source(place):
        ahead = away(place)
        near = jnp.where(ahead == 0, 0, jnp.where(ahead < half, half - 2 + ahead, count - ahead))
        return jnp.where((ahead >= half - 1) & (ahead <= half + 1), -1, near)

    rim_from, rim_row, low_last, up_last = ([-1] * count, [0] * count, [0] * count, [0] * count)
    for place, row, kinds in ((place_low, rows - RIM, low_last), (place_up, 0, up_last)):
        for value, i in ((1, (place - half + 1) % count), (0, (place + half - 1) % count)):
            assert rim_from[i] < 0
            rim_from[i] = 2 if i in (plan.over_l if value else plan.over_r) else value
            rim_row[i], kinds[i] = row, 1

    far_low, far_up = (place_low + half) % count, (place_up + half) % count
    rim_half = [int(i == far_low) for i in range(count)]
    far_half = table(rim_half, here)
    cuts = [
        [2 * int(i in plan.over_r) for i in range(count)],
        [rim_half[(i + 1) % count] for i in range(count)],
        [1 + int(i in plan.over_l) for i in range(count)],
        [1 - rim_half[(i - 1) % count] for i in range(count)],
    ]

    mode = jnp.stack(
        [
            low_far,
            up_far,
            edge_source(place_low),
            edge_source(place_up),
            far_half,
            1 - far_half,
            *(table(values, here) for values in cuts),
            over_r_kind,
            over_l_kind,
            *(table(values, here) for values in (rim_from, rim_row, low_last, up_last)),
        ]
    ).astype(I32)

    offs, info = listed(*locate(own_cols, 0), own_rows, half + 2, per_stage, bits)

    params = pltpu.CompilerParams(vmem_limit_bytes=VMEM_BYTES)
    cost = pl.CostEstimate(
        flops=2 * side * side * width * own_tiles.shape[0] // count, bytes_accessed=8 << 20, transcendentals=0
    )

    def multiply(stage, layout, sources, lists, before):
        helped = len(lists) > 2
        most = max(at + choices[0][3] if isinstance(at, int) else at[0] + 2 * at[2] for at, _, choices in layout)
        given = [*lists, mode, *sources, own_tiles] + ([received] if helped else []) + ([] if before is None else [before])
        tile_slots = lambda: pltpu.VMEM((DEPTH, UNROLL, side, side), F32)
        return pl.pallas_call(
            functools.partial(stage_kernel, stage, bits, layout, helped),
            out_shape=jax.ShapeDtypeStruct((rows, side, width), F32),
            in_specs=[SMEM] * (len(lists) + 1) + [ANY] * (len(given) - len(lists) - 1),
            out_specs=VMEM,
            scratch_shapes=[
                pltpu.VMEM((rows + 1, side, width), F32),
                pltpu.VMEM((most, side, width), F32),
                tile_slots(),
                tile_slots(),
                pltpu.SemaphoreType.DMA((len(layout) + 1,)),
                pltpu.SemaphoreType.DMA((DEPTH,)),
                pltpu.SemaphoreType.DMA((DEPTH,)),
            ],
            compiler_params=params,
            cost_estimate=cost,
            name=f"stage{stage}",
        )(*given)

    whole = lambda k: (k * rows, None, [(0, k, 0, rows)])

    def rims_early(after):
        near_shards = [sims] + from_left[1:] + from_right[1:]
        edge = jax.ShapeDtypeStruct((RIM, side, width), F32)
        low, up = pl.pallas_call(
            edge_kernel,
            out_shape=(edge, edge),
            in_specs=[SMEM] + [ANY] * (len(near_shards) + 1),
            out_specs=(VMEM, VMEM),
            scratch_shapes=[pltpu.SemaphoreType.DMA((2,))],
            compiler_params=params,
            name="edges",
        )(mode, *near_shards, after)
        apart = lambda i, k: min((i - k) % count, (k - i) % count)
        places = lambda place: [k for k in range(count) if apart(k, place) < half - 1]
        low = lax.ppermute(low, both, plan.between(1, places(place_low)))
        up = lax.ppermute(up, both, plan.between(-1, places(place_up)))
        return low, up

    from_left, from_right = [sims], [sims]
    lists, acc, shards = [offs, info], None, [sims]
    for s in range(half):
        if s == join:
            got = received[:, per_owner * side :].astype(I32)
            cols, takes, live = got[:, 0], got[:, 1], got[:, 2]
            stage, slot = locate(cols, join)
            stage = jnp.where(live > 0, stage, half + 2)
            lists = lists + list(listed(stage, slot, takes, half + 2, per_stage, bits, per_owner))
            shards = [sims] + [x for pair in zip(from_left[1:], from_right[1:]) for x in pair]
        if s < half - 1:
            last = s == half - 2
            arriving = [
                lax.ppermute(from_left[-1], "nbr", plan.last_right if last else plan.right),
                lax.ppermute(from_right[-1], "nbr", plan.last_left if last else plan.left),
            ]
            if last:
                gives_right = table([int(i in plan.from_right) for i in range(count)], here) > 0
                over = lax.ppermute(jnp.where(gives_right, from_right[-1], from_left[-1]), "nbr", plan.over)
        else:
            outgoing = pl.pallas_call(
                cut_kernel,
                out_shape=tuple(jax.ShapeDtypeStruct((n, side, width), F32) for n in (cut, cut, RIM)),
                in_specs=[SMEM] + [ANY] * 3,
                out_specs=(VMEM,) * 3,
                scratch_shapes=[pltpu.SemaphoreType.DMA((3,))],
                compiler_params=params,
                name="cut",
            )(mode, from_left[-1], from_right[-1], over)
            arriving = [lax.ppermute(x, "nbr", pairs) for x, pairs in zip(outgoing, (plan.right, plan.left))]
            near_places = lambda place: [(place + half - 1) % count, (place - half + 1) % count]
            pairs = plan.between(1, near_places(place_low)) + plan.between(-1, near_places(place_up))
            rim_last = lax.ppermute(outgoing[2], both, pairs)
        layout = [whole(k) for k in range(len(shards))]
        if s == half - 1:
            amount = len(shards)
            for k in range(2):
                at = amount - 2 + k
                layout[at] = (at * rows, OVER + k, [(0, at, 0, rows), (1, amount, 0, rows)])
            shards = shards + [over]
        acc = multiply(s, layout, shards, lists, acc)
        if s == half - 2:
            low_early, up_early = rims_early(acc)
        ties = [acc, *arriving] + ([received] if s == join - 1 else []) + ([over] if s == half - 2 else [])
        ties = lax.optimization_barrier(ties)
        acc, shards = ties[0], ties[1:3]
        if s == half - 2:
            over = ties[-1]
        if s == join - 1:
            received = ties[3]
        if s < half - 1:
            from_left.append(shards[0])
            from_right.append(shards[1])
    far_a, far_b = shards

    rim_far = lax.ppermute(far_a, both, plan.between(1, [far_low]) + plan.between(-1, [far_up]))

    layout = [
        ((0, FAR_PLACE, cut), None, [(0, 0, 0, cut)]),
        ((0, FAR_PLACE + 1, cut), None, [(0, 1, 0, cut)]),
        (rows, LAST, [(0, 2, 0, RIM), (1, 4, 0, RIM)]),
        (rows + RIM, LAST + 1, [(0, 3, 0, RIM), (1, 4, 0, RIM)]),
    ]
    acc = multiply(half, layout, [far_a, far_b, low_early, up_early, rim_last], lists, acc)
    layout = [(rows, None, [(0, 0, cut - RIM, RIM)]), (rows + RIM, None, [(0, 0, 0, RIM)])]
    return multiply(half + 1, layout, [rim_far], lists, acc)


def solution(mesh):
    spread = P(("grp", "nbr"), None, None)
    flat = P(("grp", "nbr"))
    return jax.shard_map(
        functools.partial(local, Plan(mesh)),
        mesh=mesh,
        in_specs=(spread, spread, flat, flat, spread, flat, flat, flat),
        out_specs=spread,
        check_vma=False,
    )
```

```python
import functools

import jax
import jax.numpy as jnp
import numpy as np
from jax import lax
from jax.experimental import pallas as pl
from jax.experimental.pallas import tpu as pltpu
from jax.sharding import PartitionSpec as P

RIM = 8
UNROLL = 8
NOTE_ROWS = 8
FAR_PLACE, CUTS, OVER, RIM_FROM, LAST = 4, 6, 10, 12, 14
DEPTH = 4
VMEM_BYTES = 42 << 20
F32 = jnp.float32
I32 = jnp.int32


def grid_of(mesh):
    count = mesh.shape["nbr"]
    try:
        where = np.array([d.coords for d in mesh.devices[0]])
    except AttributeError:
        return [(i, 0) for i in range(count)]
    axes = [a for a in range(where.shape[1]) if len(set(where[:, a])) > 1]
    if len(axes) != 2:
        return [(i, 0) for i in range(count)]
    first, second = axes
    if len(set(where[:, second])) > len(set(where[:, first])):
        first, second = second, first
    where = where - where.min(axis=0)
    return [(int(w[first]), int(w[second])) for w in where]


def ring_of(places):
    index = {place: n for n, place in enumerate(places)}
    rows = max(p[0] for p in places) + 1
    cols = max(p[1] for p in places) + 1
    if len(index) != rows * cols or rows % 2 or cols < 2:
        return list(range(len(places)))
    walk = [(r, 0) for r in range(rows)]
    for step, r in enumerate(reversed(range(rows))):
        across = range(1, cols) if step % 2 == 0 else reversed(range(1, cols))
        walk += [(r, c) for c in across]
    return [index[w] for w in walk]


class Plan:
    def __init__(self, mesh):
        self.groups = mesh.shape["grp"]
        self.count = mesh.shape["nbr"]
        places = grid_of(mesh)
        self.ring = ring_of(places)
        self.pos = [self.ring.index(n) for n in range(self.count)]
        self.half = self.count // 2
        count, half = self.count, self.half
        self.right = self.around([(i, (i + 1) % count) for i in range(count)])
        self.left = self.around([(i, (i - 1) % count) for i in range(count)])
        near = lambda a, b: sum(abs(u - v) for u, v in zip(places[self.ring[a]], places[self.ring[b]])) == 1
        pairs, self.over_r, self.over_l, self.from_right = [], [], [], []
        for i in range(count) if half > 3 else ():
            for members, j in ((self.over_r, (i + 3) % count), (self.over_l, (i - 3) % count)):
                if near(i, j) and all(i != b and j != a for a, b in pairs):
                    pairs.append((j, i))
                    members.append(i)
                    self.from_right += [j] if members is self.over_r else []
        self.over = self.around(pairs)
        self.last_right = self.around([((i - 1) % count, i) for i in range(count) if i not in self.over_r])
        self.last_left = self.around([((i + 1) % count, i) for i in range(count) if i not in self.over_l])

    def around(self, pairs):
        return [(self.ring[a], self.ring[b]) for a, b in pairs]

    def between(self, step, keep):
        return [
            (g * self.count + self.ring[i], (g + step) * self.count + self.ring[i])
            for g in range(self.groups)
            if 0 <= g + step < self.groups
            for i in keep
        ]


def product(a, b):
    a_hi, b_hi = a.astype(jnp.bfloat16), b.astype(jnp.bfloat16)
    a_lo = (a - a_hi.astype(F32)).astype(jnp.bfloat16)
    b_lo = (b - b_hi.astype(F32)).astype(jnp.bfloat16)
    dot = functools.partial(jnp.dot, preferred_element_type=F32)
    return dot(a_hi, b_hi) + (dot(a_lo, b_hi) + dot(a_hi, b_lo))


def run_list(offs, info, stage, bits, fetch_tile, xs, acc, buf, sems, ready):
    slot_bits, row_bits = bits
    total = info.shape[0]
    dump = acc.shape[0] - 1
    first, last = offs[stage], offs[stage + 1]
    groups = lax.div(last - first + (UNROLL - 1), UNROLL)

    def fetch(g):
        s = lax.rem(g, DEPTH)
        for u in range(UNROLL):
            at = jnp.minimum(first + g * UNROLL + u, total - 1)
            fetch_tile(lax.shift_right_logical(info[at], slot_bits + row_bits), buf.at[s, u], sems.at[s]).start()

    for g in range(DEPTH - 1):
        pl.when(g < groups)(functools.partial(fetch, jnp.int32(g)))
    ready()

    def body(g, carry):
        s = lax.rem(g, DEPTH)
        pl.when(g + DEPTH - 1 < groups)(lambda: fetch(g + DEPTH - 1))
        for u in range(UNROLL):
            fetch_tile(0, buf.at[s, u], sems.at[s]).wait()
        rows, terms = [], []
        for u in range(UNROLL):
            at = first + g * UNROLL + u
            entry = info[jnp.minimum(at, total - 1)]
            row = lax.shift_right_logical(entry, slot_bits) & ((1 << row_bits) - 1)
            slot = jnp.where(at < last, entry & ((1 << slot_bits) - 1), 0)
            rows.append(jnp.where(at < last, row, dump))
            terms.append(product(buf[s, u], xs[slot]))
        for row, term in zip(rows, terms):
            acc[row] += term
        return carry

    lax.fori_loop(0, groups, body, 0)


def stage_kernel(stage, bits, layout, helped, *refs):
    refs = list(refs)
    offs, info = refs.pop(0), refs.pop(0)
    hoffs, hinfo = (refs.pop(0), refs.pop(0)) if helped else (None, None)
    mode = refs.pop(0)
    sources = [refs.pop(0) for _ in range(1 + max(c[1] for place in layout for c in place[2]))]
    tiles = refs.pop(0)
    received = refs.pop(0) if helped else None
    before = refs.pop(0) if stage else None
    out, acc, xs, buf, hbuf, xsems, sems, hsems = refs
    rows = acc.shape[0] - 1
    kept = out.shape[0]

    def bring(at, source, start, size, sem):
        return pltpu.make_async_copy(sources[source].at[pl.ds(start, size)], xs.at[pl.ds(at, size)], sem)

    back = None
    if before is not None:
        back = pltpu.make_async_copy(before, acc.at[pl.ds(0, rows)], xsems.at[len(layout)])
        back.start()
    def place_of(at):
        return at if isinstance(at, int) else at[0] + mode[at[1]] * at[2]

    for k, (at, which, choices) in enumerate(layout):
        for value, source, start, size in choices:
            start_it = bring(place_of(at), source, start, size, xsems.at[k]).start
            if which is None:
                start_it()
            else:
                pl.when(mode[which] == value)(start_it)

    def ready():
        if back is None:
            acc[...] = jnp.zeros_like(acc)
        else:
            back.wait()
        for k, (at, _, choices) in enumerate(layout):
            _, source, start, size = choices[0]
            bring(place_of(at), source, start, size, xsems.at[k]).wait()

    def own_tile(t, place, sem):
        return pltpu.make_async_copy(tiles.at[t], place, sem)

    side = tiles.shape[1]

    def help_tile(t, place, sem):
        per = (received.shape[1] - NOTE_ROWS) // side
        chunk = lax.div(t, per)
        start = pl.multiple_of((t - chunk * per) * side, side)
        return pltpu.make_async_copy(received.at[chunk, pl.ds(start, side)], place, sem)

    run_list(offs, info, stage, bits, own_tile, xs, acc, buf, sems, ready)
    if helped:
        run_list(hoffs, hinfo, stage, bits, help_tile, xs, acc, hbuf, hsems, lambda: None)
    out[...] = acc[pl.ds(0, kept)]


def edge_kernel(mode, *refs):
    refs = list(refs)
    low, up, sems = refs[-3:]
    shards = refs[:-4]
    size = shards[0].shape[0]
    for which, out, sem in ((2, low, sems.at[0]), (3, up, sems.at[1])):
        pl.when(mode[which] < 0)(pltpu.make_async_copy(shards[0].at[pl.ds(0, RIM)], out, sem).start)

    def pick(k, ref):
        @pl.when(mode[2] == k)
        def _():
            pltpu.make_async_copy(ref.at[pl.ds(size - RIM, RIM)], low, sems.at[0]).start()

        @pl.when(mode[3] == k)
        def _():
            pltpu.make_async_copy(ref.at[pl.ds(0, RIM)], up, sems.at[1]).start()

    for k, ref in enumerate(shards):
        pick(k, ref)
    pltpu.make_async_copy(shards[0].at[pl.ds(0, RIM)], low, sems.at[0]).wait()
    pltpu.make_async_copy(shards[0].at[pl.ds(0, RIM)], up, sems.at[1]).wait()


def cut_kernel(mode, *refs):
    *shards, first, second, rim, sems = refs
    half = first.shape[0]
    outs = [(first, mode[CUTS], mode[CUTS + 1] * half), (second, mode[CUTS + 2], mode[CUTS + 3] * half)]
    outs.append((rim, jnp.maximum(mode[RIM_FROM], 0), mode[RIM_FROM + 1]))
    for k, (out, which, start) in enumerate(outs):
        for value, ref in enumerate(shards):
            copy = pltpu.make_async_copy(ref.at[pl.ds(start, out.shape[0])], out, sems.at[k])
            pl.when(which == value)(copy.start)
    for k, (out, _, _) in enumerate(outs):
        pltpu.make_async_copy(shards[0].at[pl.ds(0, out.shape[0])], out, sems.at[k]).wait()


def bits_for(n):
    return max(1, (n - 1).bit_length())


SMEM = pl.BlockSpec(memory_space=pltpu.SMEM)
ANY = pl.BlockSpec(memory_space=pl.ANY)
VMEM = pl.BlockSpec(memory_space=pltpu.VMEM)


def table(values, index):
    return sum(jnp.where(index == k, I32(v), I32(0)) for k, v in enumerate(values))


def listed(stage, slot, row, stages, per_stage, bits, kept=None):
    place = stage * per_stage + slot
    rest = (row << bits[0]) | slot
    if kept is not None:
        place, rest = (x[:, :kept].reshape(-1) for x in (place, rest))
    total = place.shape[0]
    number = jnp.arange(total, dtype=I32)
    key = place * total + number
    rank = jnp.sum((key[None, :] < key[:, None]).astype(I32), axis=1)
    entry = (number << (bits[0] + bits[1])) | rest
    info = jnp.sum(jnp.where(rank[:, None] == number[None, :], entry[:, None], 0), axis=0)
    starts = jnp.arange(stages + 1, dtype=I32) * per_stage
    offs = jnp.sum((place[None, :] < starts[:, None]).astype(I32), axis=1)
    return offs, info


def local(plan, sims, own_tiles, own_cols, own_rows, help_tiles, help_cols, help_rows, help_live):
    rows, side, width = sims.shape
    count, half = plan.count, plan.half
    group_rows = rows * count
    cut = rows // 2
    assert rows == 2 * cut and cut >= RIM
    slots = help_tiles.shape[0]
    per_owner = slots // count
    join = min(3, half - 1)
    per_stage = (2 * join + 1) * rows + 2 * RIM
    bits = (bits_for(per_stage), bits_for(rows))
    both = ("grp", "nbr")
    here = table(plan.pos, lax.axis_index("nbr"))

    notes = jnp.stack([help_cols, help_rows, help_live], axis=0).astype(F32).reshape(3, count, per_owner)
    notes = jnp.pad(notes.transpose(1, 0, 2), ((0, 0), (0, NOTE_ROWS - 3), (0, width - per_owner)))
    sent = jnp.concatenate([help_tiles.reshape(count, per_owner * side, width), notes], axis=1)
    received = lax.all_to_all(sent, "nbr", split_axis=0, concat_axis=0, tiled=True)

    place_low, place_up = plan.pos[count - 1], plan.pos[0]

    def away(place):
        return lax.rem(I32(place) - here + count, I32(count))

    low_far = (away(place_low) == half).astype(I32)
    up_far = (away(place_up) == half).astype(I32)

    def locate(cols, least):
        block = cols - RIM
        low, up = block < 0, block >= group_rows
        inside = jnp.clip(block, 0, group_rows - 1)
        shard = inside // rows
        ahead = lax.rem(table(plan.pos, shard) - here + count, I32(count))
        near = jnp.minimum(ahead, count - ahead)
        stage = jnp.maximum(near, least)
        right = ((ahead > 0) & (ahead < half)).astype(I32)
        order = jnp.where(stage == join, jnp.where(near == 0, 0, 2 * near - 1 + right), right)
        slot = inside - shard * rows + order * rows
        slot = jnp.where(low, rows + cols, jnp.where(up, rows + RIM + block - group_rows, slot))
        stage = jnp.where(low, half + low_far, jnp.where(up, half + up_far, stage))
        return stage, slot

    over_r_kind = table([int(i in plan.over_r) for i in range(count)], here)
    over_l_kind = table([int(i in plan.over_l) for i in range(count)], here)

    def edge_source(place):
        ahead = away(place)
        near = jnp.where(ahead == 0, 0, jnp.where(ahead < half, half - 2 + ahead, count - ahead))
        return jnp.where((ahead >= half - 1) & (ahead <= half + 1), -1, near)

    rim_from, rim_row, low_last, up_last = ([-1] * count, [0] * count, [0] * count, [0] * count)
    for place, row, kinds in ((place_low, rows - RIM, low_last), (place_up, 0, up_last)):
        for value, i in ((1, (place - half + 1) % count), (0, (place + half - 1) % count)):
            assert rim_from[i] < 0
            rim_from[i] = 2 if i in (plan.over_l if value else plan.over_r) else value
            rim_row[i], kinds[i] = row, 1

    far_low, far_up = (place_low + half) % count, (place_up + half) % count
    rim_half = [int(i == far_low) for i in range(count)]
    far_half = table(rim_half, here)
    cuts = [
        [2 * int(i in plan.over_r) for i in range(count)],
        [rim_half[(i + 1) % count] for i in range(count)],
        [1 + int(i in plan.over_l) for i in range(count)],
        [1 - rim_half[(i - 1) % count] for i in range(count)],
    ]

    mode = jnp.stack(
        [
            low_far,
            up_far,
            edge_source(place_low),
            edge_source(place_up),
            far_half,
            1 - far_half,
            *(table(values, here) for values in cuts),
            over_r_kind,
            over_l_kind,
            *(table(values, here) for values in (rim_from, rim_row, low_last, up_last)),
        ]
    ).astype(I32)

    offs, info = listed(*locate(own_cols, 0), own_rows, half + 2, per_stage, bits)

    params = pltpu.CompilerParams(vmem_limit_bytes=VMEM_BYTES)
    cost = pl.CostEstimate(
        flops=2 * side * side * width * own_tiles.shape[0] // count, bytes_accessed=8 << 20, transcendentals=0
    )

    def multiply(stage, layout, sources, lists, before):
        helped = len(lists) > 2
        most = max(at + choices[0][3] if isinstance(at, int) else at[0] + 2 * at[2] for at, _, choices in layout)
        given = [*lists, mode, *sources, own_tiles] + ([received] if helped else []) + ([] if before is None else [before])
        tile_slots = lambda: pltpu.VMEM((DEPTH, UNROLL, side, side), F32)
        return pl.pallas_call(
            functools.partial(stage_kernel, stage, bits, layout, helped),
            out_shape=jax.ShapeDtypeStruct((rows, side, width), F32),
            in_specs=[SMEM] * (len(lists) + 1) + [ANY] * (len(given) - len(lists) - 1),
            out_specs=VMEM,
            scratch_shapes=[
                pltpu.VMEM((rows + 1, side, width), F32),
                pltpu.VMEM((most, side, width), F32),
                tile_slots(),
                tile_slots(),
                pltpu.SemaphoreType.DMA((len(layout) + 1,)),
                pltpu.SemaphoreType.DMA((DEPTH,)),
                pltpu.SemaphoreType.DMA((DEPTH,)),
            ],
            compiler_params=params,
            cost_estimate=cost,
            name=f"stage{stage}",
        )(*given)

    whole = lambda k: (k * rows, None, [(0, k, 0, rows)])

    def rims_early(after):
        near_shards = [sims] + from_left[1:] + from_right[1:]
        edge = jax.ShapeDtypeStruct((RIM, side, width), F32)
        low, up = pl.pallas_call(
            edge_kernel,
            out_shape=(edge, edge),
            in_specs=[SMEM] + [ANY] * (len(near_shards) + 1),
            out_specs=(VMEM, VMEM),
            scratch_shapes=[pltpu.SemaphoreType.DMA((2,))],
            compiler_params=params,
            name="edges",
        )(mode, *near_shards, after)
        apart = lambda i, k: min((i - k) % count, (k - i) % count)
        places = lambda place: [k for k in range(count) if apart(k, place) < half - 1]
        low = lax.ppermute(low, both, plan.between(1, places(place_low)))
        up = lax.ppermute(up, both, plan.between(-1, places(place_up)))
        return low, up

    from_left, from_right = [sims], [sims]
    lists, acc, shards = [offs, info], None, [sims]
    for s in range(half):
        if s == join:
            got = received[:, per_owner * side :].astype(I32)
            cols, takes, live = got[:, 0], got[:, 1], got[:, 2]
            stage, slot = locate(cols, join)
            stage = jnp.where(live > 0, stage, half + 2)
            lists = lists + list(listed(stage, slot, takes, half + 2, per_stage, bits, per_owner))
            shards = [sims] + [x for pair in zip(from_left[1:], from_right[1:]) for x in pair]
        if s < half - 1:
            last = s == half - 2
            arriving = [
                lax.ppermute(from_left[-1], "nbr", plan.last_right if last else plan.right),
                lax.ppermute(from_right[-1], "nbr", plan.last_left if last else plan.left),
            ]
            if last:
                gives_right = table([int(i in plan.from_right) for i in range(count)], here) > 0
                over = lax.ppermute(jnp.where(gives_right, from_right[-1], from_left[-1]), "nbr", plan.over)
        else:
            outgoing = pl.pallas_call(
                cut_kernel,
                out_shape=tuple(jax.ShapeDtypeStruct((n, side, width), F32) for n in (cut, cut, RIM)),
                in_specs=[SMEM] + [ANY] * 3,
                out_specs=(VMEM,) * 3,
                scratch_shapes=[pltpu.SemaphoreType.DMA((3,))],
                compiler_params=params,
                name="cut",
            )(mode, from_left[-1], from_right[-1], over)
            arriving = [lax.ppermute(x, "nbr", pairs) for x, pairs in zip(outgoing, (plan.right, plan.left))]
            near_places = lambda place: [(place + half - 1) % count, (place - half + 1) % count]
            pairs = plan.between(1, near_places(place_low)) + plan.between(-1, near_places(place_up))
            rim_last = lax.ppermute(outgoing[2], both, pairs)
        layout = [whole(k) for k in range(len(shards))]
        if s == half - 1:
            amount = len(shards)
            for k in range(2):
                at = amount - 2 + k
                layout[at] = (at * rows, OVER + k, [(0, at, 0, rows), (1, amount, 0, rows)])
            shards = shards + [over]
        acc = multiply(s, layout, shards, lists, acc)
        if s == half - 2:
            low_early, up_early = rims_early(acc)
        if s == half - 1:
            acc, far_a = lax.optimization_barrier((acc, arriving[0]))
            far_b = arriving[1]
            break
        ties = [acc, *arriving] + ([received] if s == join - 1 else []) + ([over] if s == half - 2 else [])
        ties = lax.optimization_barrier(ties)
        acc, shards = ties[0], ties[1:3]
        if s == half - 2:
            over = ties[-1]
        if s == join - 1:
            received = ties[3]
        if s < half - 1:
            from_left.append(shards[0])
            from_right.append(shards[1])

    rim_far = lax.ppermute(far_a, both, plan.between(1, [far_low]) + plan.between(-1, [far_up]))

    layout = [
        ((0, FAR_PLACE, cut), None, [(0, 0, 0, cut)]),
        ((0, FAR_PLACE + 1, cut), None, [(0, 1, 0, cut)]),
        (rows, LAST, [(0, 2, 0, RIM), (1, 4, 0, RIM)]),
        (rows + RIM, LAST + 1, [(0, 3, 0, RIM), (1, 4, 0, RIM)]),
    ]
    acc = multiply(half, layout, [far_a, far_b, low_early, up_early, rim_last], lists, acc)
    layout = [(rows, None, [(0, 0, cut - RIM, RIM)]), (rows + RIM, None, [(0, 0, 0, RIM)])]
    return multiply(half + 1, layout, [rim_far], lists, acc)


def solution(mesh):
    spread = P(("grp", "nbr"), None, None)
    flat = P(("grp", "nbr"))
    return jax.shard_map(
        functools.partial(local, Plan(mesh)),
        mesh=mesh,
        in_specs=(spread, spread, flat, flat, spread, flat, flat, flat),
        out_specs=spread,
        check_vma=False,
    )
```
